32 devices in a mesh: groups: 2 (over x), vec: 16 (over z, y, core).
Axes of the slice: x: 2, y: 2, z: 4, core: 2. Of those that a mesh axis runs over, the one named last changes fastest.
Arguments:
- walkers: bfloat16 [32, 48, 1200], P(('groups', 'vec')), parts along dimension 0, may hold values from -6 to 6, as said below
- points: bfloat16 [2400, 2560], P('groups'), parts along dimension 0, may hold values from -0.1875 to 0.1875
- cholesky: bfloat16 [19200, 2560], P(('groups', 'vec')), parts along dimension 0, may hold values from -1.1953125 to 1.1953125
- field_draws: float32 [32, 9600], P('groups', 'vec'), parts along dimension 0, may hold values from -6 to 6
- counts: int32 [32], P(('groups', 'vec')), parts along dimension 0, may hold values from 0 to 3, as said below
- slot_map: int32 [32], P(('groups', 'vec')), parts along dimension 0, may hold values from 0 to 15, as said below
Outputs:
- walkers_next: bfloat16 [32, 48, 1200], P(('groups', 'vec')), parts along dimension 0
- shifts: float32 [32, 9600], P('groups', 'vec'), parts along dimension 0
The draws below stay inside these ranges and needn't reach their ends.
There are 2 independent parts, one for each index of `groups`. The reference program is written for one: setup_inputs(seed, part) draws one part's arguments, and reference() takes and returns one part's arrays. A program takes and returns all parts, laid end to end along the dimension named above; each array names one. Nothing has to cross between parts.
Inputs may be any that keep to these rules, and one draw needn't show every extreme that they name: The counts sum to 16. `slot_map`: A permutation of the 16 rows. The copies of the walkers of one device (rows k * 1 to k + 1 - 1 of the walkers) land in at most one row of each device. `walkers`: each walker's first 48 columns have diagonal entries in [2, 3] and off-diagonal entries below 1.5 / 48 in magnitude.
All inputs are finite; a program needn't handle non-finite values.
Results may differ from the reference program's by a relative error of at most 0.025.
Values may be sent and summed in bfloat16 or wider, within the bound.
A program may use at most 64 MiB of HBM per device.

```python
import jax
import jax.numpy as jnp
from jax import lax

NORB = 1200
NE = 48
NCHOL = 9600
NPTS = 2560
WALK_DEV = 1
ORDER = 4
WALKERS = 16


def draw_walkers(key, part):
    key = jax.random.fold_in(key, 11)
    first, second, third = jax.random.split(key, 3)
    diagonal = jax.random.uniform(first, (WALKERS, NE), jnp.float32, 2.0, 3.0)
    offside = jax.random.uniform(second, (WALKERS, NE, NE), jnp.float32, -1.5 / NE, 1.5 / NE)
    identity = jnp.eye(NE, dtype=jnp.float32)
    square = offside * (1.0 - identity) + identity * diagonal[:, :, None]
    remainder = jax.random.truncated_normal(third, -6.0, 6.0, (WALKERS, NE, NORB - NE), jnp.float32)
    return jnp.concatenate([square, remainder], axis=-1).astype(jnp.bfloat16)


def draw_counts(key, part):
    key = jax.random.fold_in(key, 23)
    shuffled = jax.random.permutation(key, WALKERS).astype(jnp.int32)
    quarter = WALKERS // 4
    eighth = WALKERS // 8
    counts = jnp.ones((WALKERS,), jnp.int32)
    counts = counts.at[shuffled[:quarter]].set(0)
    counts = counts.at[shuffled[quarter:quarter + eighth]].set(3)
    return counts


def draw_slot_map(key, part):
    key = jax.random.fold_in(key, 37)
    first, second = jax.random.split(key)
    devices = WALKERS // WALK_DEV
    device_order = jax.random.permutation(first, devices).astype(jnp.int32)
    slot_order = jax.random.permutation(second, WALK_DEV).astype(jnp.int32)
    positions = jnp.arange(WALKERS, dtype=jnp.int32)
    return device_order[positions % devices] * WALK_DEV + slot_order[positions // devices]


def shard_levels(stream_key, dims, shards, smallest, high):
    level, own = 1.0, jax.random.fold_in(stream_key, 6)
    for position, blocks in shards:
        steps = jnp.exp(jax.random.uniform(jax.random.fold_in(own, position), (blocks,), jnp.float32, smallest / len(shards), high / len(shards)))
        level = level * jnp.repeat(steps, dims[position] // blocks).reshape([-1 if axis == position else 1 for axis in range(len(dims))])
    return level


def centred(key, shape, width, limit, pieces=(), kind=jnp.bfloat16):
    drawn = jax.random.normal(key, shape, jnp.float32) * width
    if len(pieces) > 0:
        drawn = shard_levels(key, shape, pieces, -0.22, 0.18) * drawn
    return jnp.clip(drawn, min=-limit, max=limit).astype(kind)


def setup_inputs(seed: int = 0, part: int = 0) -> dict:
    keys = jax.random.split(jax.random.key(seed), 7)
    part_splits = jax.random.split(jax.random.fold_in(keys[6], part), 7)
    walkers = draw_walkers(jax.random.fold_in(jax.random.fold_in(keys[6], part), 71), part)
    points = centred(part_splits[1], (NORB, NPTS), NORB ** -0.5, 0.1875)
    cholesky = centred(part_splits[2], (NCHOL, NPTS), 0.2, 1.1953125, ((0, 16),))
    field_draws = centred(part_splits[3], (WALKERS, NCHOL), 1.0, 6.0, ((1, 16),), jnp.float32)
    counts = draw_counts(jax.random.fold_in(jax.random.fold_in(keys[6], part), 71), part)
    slot_map = draw_slot_map(jax.random.fold_in(jax.random.fold_in(keys[6], part), 71), part)
    return {"walkers": walkers, "points": points, "cholesky": cholesky, "field_draws": field_draws, "counts": counts, "slot_map": slot_map}


tau_root = 0.03
highest = lax.Precision.HIGHEST

def green_row(walker, points):
    electrons = walker.shape[0]
    square = walker[:, :electrons]
    gram = jnp.dot(square.T.astype(jnp.float32), square.astype(jnp.float32), preferred_element_type=jnp.float32)
    right_side = jnp.dot(square.T.astype(jnp.float32), walker.astype(jnp.float32), preferred_element_type=jnp.float32)
    factor = jnp.linalg.cholesky(gram)
    theta = jax.scipy.linalg.cho_solve((factor, True), right_side).astype(jnp.bfloat16)
    projected = jnp.dot(theta.astype(jnp.float32), points.astype(jnp.float32), preferred_element_type=jnp.float32)
    return jnp.sum(projected * points[:electrons].astype(jnp.float32), axis=0).astype(jnp.bfloat16)

def propagate_one(walker, weight_row, points):
    term_now = walker
    total = walker.astype(jnp.float32)
    for order_index in range(1, ORDER + 1):
        projected = jnp.dot(term_now.astype(jnp.float32), points.astype(jnp.float32), preferred_element_type=jnp.float32)
        scaled = (projected * weight_row[None, :]).astype(jnp.bfloat16)
        back = jnp.dot(scaled.astype(jnp.float32), points.T.astype(jnp.float32), preferred_element_type=jnp.float32) / order_index
        total = total + back
        term_now = back.astype(jnp.bfloat16)
    return total.astype(jnp.bfloat16)

def reference(walkers, points, cholesky, field_draws, counts, slot_map):
    gbar = lax.map(lambda walker: green_row(walker, points), walkers)
    bias = jnp.dot(gbar.astype(jnp.float32), cholesky.T.astype(jnp.float32), preferred_element_type=jnp.float32)
    shifts = jnp.clip(bias, -1.0, 1.0)
    fields = (field_draws - shifts).astype(jnp.bfloat16)
    weights = tau_root * jnp.dot(fields.astype(jnp.float32), cholesky.astype(jnp.float32), preferred_element_type=jnp.float32)
    propagated = lax.map(lambda pair: propagate_one(pair[0], pair[1], points), (walkers, weights))
    total_rows = counts.shape[0]
    ends = jnp.cumsum(counts).astype(jnp.int32)
    positions = jnp.arange(total_rows, dtype=jnp.int32)
    source = jnp.sum((ends[None, :] <= positions[:, None]).astype(jnp.int32), axis=1).astype(jnp.int32)
    inverse = jnp.zeros((total_rows,), jnp.int32).at[slot_map].set(positions)
    walkers_next = propagated[source[inverse]]
    return (walkers_next, shifts)
```

```python
import functools
import math

import jax
import jax.numpy as jnp
from jax import lax
from jax.experimental import pallas as pl
from jax.experimental.pallas import tpu as pltpu
from jax.sharding import PartitionSpec as P

ORDER = 4
TAU_ROOT = 0.03
LANES = 128
ROWS = 16
F32 = jnp.float32
BF16 = jnp.bfloat16
MESH = pl.DeviceIdType.MESH


def dot(a, b):
    return lax.dot_general(a, b, (((1,), (0,)), ((), ())), preferred_element_type=F32)


def dot_nt(a, b):
    return lax.dot_general(a, b, (((1,), (1,)), ((), ())), preferred_element_type=F32)


def dot_tn(a, b):
    return lax.dot_general(a, b, (((0,), (0,)), ((), ())), preferred_element_type=F32)


def split(value):
    high = value.astype(BF16)
    return high, (value - high.astype(F32)).astype(BF16)


def inverse_of(square):
    size = square.shape[0]
    row = lax.broadcasted_iota(jnp.int32, (size, size), 0)
    col = lax.broadcasted_iota(jnp.int32, (size, size), 1)
    eye = row == col
    one = jnp.where(eye, 1.0, 0.0).astype(F32)
    wide = square.astype(F32)
    diagonal = jnp.where(eye, wide, 0.0)
    down = 1.0 / jnp.sum(diagonal, axis=1, keepdims=True)
    across = 1.0 / jnp.sum(diagonal, axis=0, keepdims=True)
    power = jnp.where(eye, 0.0, -wide * down)
    series = one + power
    for _ in range(4):
        low = power.astype(BF16)
        power = dot(low, low)
        series = series + dot(series.astype(BF16), power.astype(BF16))
    guess = series * across
    twice = jnp.concatenate([square, square], axis=1)
    for _ in range(2):
        high, low = split(guess)
        residual = one - dot(twice, jnp.concatenate([high, low], axis=0))
        guess = guess + dot(high, residual.astype(BF16))
    return guess


def kernel(
    sizes,
    counts_ref, slots_ref, walk_ref, draws_ref, points_hbm, chol_hbm,
    out_ref, shift_ref,
    pts, chol, xsend, stash, selected, xrecv, gbar32, gsend, grecv, gwide, gmat,
    psum32, psend, precv, proj, proj_next, scaled, term, total, weight,
    load_sem, a_send, a_recv, b_send, b_recv, c_send, c_recv, d_send, d_recv,
):
    n, tiles, electrons, orbitals, npts, prow = sizes
    me = lax.axis_index("vec")
    group = lax.axis_index("groups")
    row_tiles = electrons // ROWS
    col_tiles = -(-orbitals // LANES)
    pieces = npts // LANES
    width = tiles * LANES
    chunk = math.gcd(npts, 512)

    load_points = pltpu.make_async_copy(points_hbm, pts, load_sem.at[0])
    load_points.start()
    load_chol = pltpu.make_async_copy(chol_hbm, chol, load_sem.at[1])
    load_chol.start()

    barrier = pltpu.get_barrier_semaphore()

    def greet(step, carry):
        pl.semaphore_signal(
            barrier, inc=1, device_id=(group, lax.rem(me + step, n)), device_id_type=MESH
        )
        return carry

    lax.fori_loop(1, n, greet, 0)

    lane = lax.broadcasted_iota(jnp.int32, (ROWS, LANES), 1)
    meta = jnp.where(lane < LANES // 2, counts_ref[0], slots_ref[0]).astype(F32).astype(BF16)
    for relay in range(n):
        for t in range(tiles):
            tile = relay * tiles + t
            if tile < row_tiles * col_tiles:
                r, c = tile // col_tiles, tile % col_tiles
                low, high = c * LANES, min(orbitals, (c + 1) * LANES)
                block = walk_ref[r * ROWS:(r + 1) * ROWS, low:high]
                if high - low < LANES:
                    block = jnp.concatenate(
                        [block, jnp.zeros((ROWS, LANES - (high - low)), BF16)], axis=1
                    )
                xsend[relay, :, t * LANES:(t + 1) * LANES] = block
            else:
                xsend[relay, :, t * LANES:(t + 1) * LANES] = jnp.zeros((ROWS, LANES), BF16)
        xsend[relay, :, width:] = meta

    pl.semaphore_wait(barrier, n - 1)

    def rows_at(index, rows):
        return pl.ds(pl.multiple_of(index * rows, rows), rows)

    def copy_a(step):
        peer = lax.rem(me + step, n)
        return pltpu.make_async_remote_copy(
            src_ref=xsend.at[peer], dst_ref=stash.at[rows_at(me, ROWS)],
            send_sem=a_send.at[step], recv_sem=a_recv.at[step],
            device_id=(group, peer), device_id_type=MESH,
        )

    def copy_b(step):
        peer = lax.rem(me + step, n)
        return pltpu.make_async_remote_copy(
            src_ref=gsend, dst_ref=grecv.at[rows_at(me, prow)],
            send_sem=b_send.at[step], recv_sem=b_recv.at[step],
            device_id=(group, peer), device_id_type=MESH,
        )

    def copy_c(step):
        peer = lax.rem(me + step, n)
        return pltpu.make_async_remote_copy(
            src_ref=psend.at[rows_at(peer, prow)], dst_ref=precv.at[rows_at(me, prow)],
            send_sem=c_send.at[step], recv_sem=c_recv.at[step],
            device_id=(group, peer), device_id_type=MESH,
        )

    def copy_d(step):
        peer = lax.rem(me + step, n)
        return pltpu.make_async_remote_copy(
            src_ref=selected.at[rows_at(peer, ROWS)], dst_ref=xrecv.at[rows_at(me, ROWS)],
            send_sem=d_send.at[step], recv_sem=d_recv.at[step],
            device_id=(group, peer), device_id_type=MESH,
        )

    def start_all(make):
        def body(step, carry):
            make(step).start()
            return carry

        lax.fori_loop(1, n, body, 0)

    def arrived_all(make):
        def body(step, carry):
            make(step).wait_recv()
            return carry

        lax.fori_loop(1, n, body, 0)

    def sent_all(make):
        def body(step, carry):
            make(step).wait_send()
            return carry

        lax.fori_loop(1, n, body, 0)

    start_all(copy_a)
    stash[rows_at(me, ROWS), :] = xsend[me]

    inverse = inverse_of(walk_ref[:, :electrons])
    inv_high, inv_low = split(inverse)
    stacked = jnp.concatenate([inv_high, inv_high, inv_low], axis=1)
    load_points.wait()

    def project(source_ref, target_ref):
        def body(c, carry):
            at = pl.ds(pl.multiple_of(c * chunk, chunk), chunk)
            target_ref[:, at] = dot(source_ref[:, :orbitals], pts[:, at])
            return carry

        lax.fori_loop(0, npts // chunk, body, 0)

    project(walk_ref, proj)
    gbar32[...] = jnp.zeros_like(gbar32)
    for c in range(npts // chunk):
        at = slice(c * chunk, (c + 1) * chunk)
        high, low = split(proj[:, at])
        theta_points = dot(stacked, jnp.concatenate([high, low, high], axis=0))
        density = jnp.sum(
            theta_points * pts[:electrons, at].astype(F32), axis=0, keepdims=True
        )
        for j in range(chunk // LANES):
            k = c * (chunk // LANES) + j
            gbar32[k:k + 1, :] = density[:, j * LANES:(j + 1) * LANES]
    gsend[...] = gbar32[...].astype(BF16)
    start_all(copy_b)
    grecv[rows_at(me, prow), :] = gsend[...]

    arrived_all(copy_a)
    count_rows = stash[:, width:]
    big = n * ROWS
    i0 = lax.broadcasted_iota(jnp.int32, (big, big), 0)
    i1 = lax.broadcasted_iota(jnp.int32, (big, big), 1)
    before = jnp.where((i1 // ROWS <= i0 // ROWS) & (i1 % ROWS == 0), 1.0, 0.0).astype(BF16)
    ends = dot(before, count_rows)[:, :1]
    slot_col = count_rows[:, LANES // 2:LANES // 2 + 1].astype(F32)
    first = i0 % ROWS == 0
    place = (i0 // ROWS).astype(F32)

    wanted = (i1 // ROWS).astype(F32)
    copy_row = jnp.sum(jnp.where(first & (slot_col == wanted), place, 0.0), axis=0, keepdims=True)
    source = jnp.sum(jnp.where(first & (ends <= copy_row), 1.0, 0.0), axis=0, keepdims=True)
    pick = jnp.where((place == source) & (i0 % ROWS == i1 % ROWS), 1.0, 0.0).astype(BF16)
    selected[...] = dot_tn(pick, stash[:, :width]).astype(BF16)
    start_all(copy_d)
    xrecv[rows_at(me, ROWS), :] = selected[rows_at(me, ROWS), :]

    ones = (n, n)
    j1 = lax.broadcasted_iota(jnp.int32, (big, n), 1).astype(F32)
    k0 = lax.broadcasted_iota(jnp.int32, (big, n), 0)
    thin_first = k0 % ROWS == 0
    thin_copy = jnp.sum(
        jnp.where(thin_first & (slot_col == j1), (k0 // ROWS).astype(F32), 0.0),
        axis=0, keepdims=True,
    )
    thin_source = jnp.sum(
        jnp.where(thin_first & (ends <= thin_copy), 1.0, 0.0), axis=0, keepdims=True
    )
    thin_pick = jnp.where(
        lax.broadcasted_iota(jnp.int32, ones, 0).astype(F32) == thin_source, 1.0, 0.0
    ).astype(BF16)

    load_chol.wait()
    arrived_all(copy_b)
    gwide[...] = grecv[...].astype(F32)
    for j in range(pieces):
        gmat[:, j * LANES:(j + 1) * LANES] = gwide[pl.ds(j, n, stride=prow), :].astype(BF16)
    shifts = jnp.clip(dot_nt(gmat[...], chol[...]), -1.0, 1.0)
    shift_ref[...] = shifts
    fields = (draws_ref[...] - shifts).astype(BF16)
    fields = dot_tn(thin_pick, fields).astype(BF16)
    psum32[...] = jnp.zeros_like(psum32)
    for c in range(npts // chunk):
        part = dot(fields, chol[:, c * chunk:(c + 1) * chunk])
        for j in range(chunk // LANES):
            k = c * (chunk // LANES) + j
            psum32[pl.ds(k, n, stride=prow), :] = part[:, j * LANES:(j + 1) * LANES]
    psend[...] = psum32[...].astype(BF16)
    start_all(copy_c)
    own = psum32[rows_at(me, prow), :]

    arrived_all(copy_d)
    for tile in range(row_tiles * col_tiles):
        relay, t = tile // tiles, tile % tiles
        r, c = tile // col_tiles, tile % col_tiles
        low, high = c * LANES, min(orbitals, (c + 1) * LANES)
        block = xrecv[relay * ROWS:(relay + 1) * ROWS, t * LANES:t * LANES + high - low]
        term[r * ROWS:(r + 1) * ROWS, low:high] = block
    total[...] = term[...].astype(F32)
    project(term, proj_next)

    arrived_all(copy_c)
    precv[rows_at(me, prow), :] = jnp.zeros((prow, LANES), BF16)

    def add(w, carry):
        return carry + precv[rows_at(w, prow), :].astype(F32)

    weight[...] = TAU_ROOT * lax.fori_loop(0, n, add, own)

    def scale():
        for j in range(pieces):
            at = slice(j * LANES, (j + 1) * LANES)
            scaled[:, at] = (proj_next[:, at] * weight[j:j + 1, :]).astype(BF16)

    def back(k):
        for low in range(0, orbitals, 256):
            high = min(orbitals, low + 256)
            value = dot_nt(scaled[...], pts[low:high, :]) / k
            total[:, low:high] = total[:, low:high] + value
            term[:, low:high] = value.astype(BF16)

    def taylor(k, carry):
        scale()
        back(k.astype(F32))
        project(term, proj_next)
        return carry

    lax.fori_loop(1, ORDER, taylor, 0)
    scale()
    back(float(ORDER))
    out_ref[...] = total[...].astype(BF16)

    sent_all(copy_a)
    sent_all(copy_b)
    sent_all(copy_c)
    sent_all(copy_d)


def local(walkers, points, cholesky, field_draws, counts, slot_map):
    n = lax.axis_size("vec")
    walk_rows, electrons, orbitals = walkers.shape
    assert walk_rows == 1 and electrons % ROWS == 0
    npts = points.shape[1]
    tile_count = (electrons // ROWS) * (-(-orbitals // LANES))
    tiles = -(-tile_count // n)
    pieces = npts // LANES
    prow = -(-pieces // ROWS) * ROWS
    sizes = (n, tiles, electrons, orbitals, npts, prow)
    width = tiles * LANES
    vmem = pl.BlockSpec(memory_space=pltpu.VMEM)
    smem = pl.BlockSpec(memory_space=pltpu.SMEM)
    hbm = pl.BlockSpec(memory_space=pl.ANY)
    dma = pltpu.SemaphoreType.DMA
    walkers_next, shifts = pl.pallas_call(
        functools.partial(kernel, sizes),
        out_shape=(
            jax.ShapeDtypeStruct((electrons, orbitals), BF16),
            jax.ShapeDtypeStruct(field_draws.shape, F32),
        ),
        in_specs=[smem, smem, vmem, vmem, hbm, hbm],
        out_specs=(vmem, vmem),
        scratch_shapes=[
            pltpu.VMEM(points.shape, BF16),
            pltpu.VMEM(cholesky.shape, BF16),
            pltpu.VMEM((n, ROWS, width + LANES), BF16),
            pltpu.VMEM((n * ROWS, width + LANES), BF16),
            pltpu.VMEM((n * ROWS, width), BF16),
            pltpu.VMEM((n * ROWS, width), BF16),
            pltpu.VMEM((prow, LANES), F32),
            pltpu.VMEM((prow, LANES), BF16),
            pltpu.VMEM((n * prow, LANES), BF16),
            pltpu.VMEM((n * prow, LANES), F32),
            pltpu.VMEM((n, npts), BF16),
            pltpu.VMEM((n * prow, LANES), F32),
            pltpu.VMEM((n * prow, LANES), BF16),
            pltpu.VMEM((n * prow, LANES), BF16),
            pltpu.VMEM((electrons, npts), F32),
            pltpu.VMEM((electrons, npts), F32),
            pltpu.VMEM((electrons, npts), BF16),
            pltpu.VMEM((electrons, orbitals), BF16),
            pltpu.VMEM((electrons, orbitals), F32),
            pltpu.VMEM((prow, LANES), F32),
            dma((2,)),
        ] + [dma((n,))] * 8,
        compiler_params=pltpu.CompilerParams(
            collective_id=0, has_side_effects=True, vmem_limit_bytes=48 * 1024 * 1024
        ),
        cost_estimate=pl.CostEstimate(
            flops=2 * electrons * orbitals * npts * 9 + 4 * cholesky.size * n,
            bytes_accessed=2 * (points.size + cholesky.size),
            transcendentals=0,
        ),
    )(counts, slot_map, walkers[0], field_draws, points, cholesky)
    return walkers_next[None], shifts


def solution(mesh):
    placed = (
        P(("groups", "vec"), None, None),
        P("groups", None),
        P(("groups", "vec"), None),
        P("groups", "vec"),
        P(("groups", "vec")),
        P(("groups", "vec")),
    )
    return jax.shard_map(
        local,
        mesh=mesh,
        in_specs=placed,
        out_specs=(P(("groups", "vec"), None, None), P("groups", "vec")),
        check_vma=False,
    )
```

```python
import functools
import math

import jax
import jax.numpy as jnp
from jax import lax
from jax.experimental import pallas as pl
from jax.experimental.pallas import tpu as pltpu
from jax.sharding import PartitionSpec as P

ORDER = 4
TAU_ROOT = 0.03
LANES = 128
ROWS = 16
F32 = jnp.float32
BF16 = jnp.bfloat16
MESH = pl.DeviceIdType.MESH


def dot(a, b):
    return lax.dot_general(a, b, (((1,), (0,)), ((), ())), preferred_element_type=F32)


def dot_nt(a, b):
    return lax.dot_general(a, b, (((1,), (1,)), ((), ())), preferred_element_type=F32)


def dot_tn(a, b):
    return lax.dot_general(a, b, (((0,), (0,)), ((), ())), preferred_element_type=F32)


def split(value):
    high = value.astype(BF16)
    return high, (value - high.astype(F32)).astype(BF16)


def inverse_of(square):
    size = square.shape[0]
    row = lax.broadcasted_iota(jnp.int32, (size, size), 0)
    col = lax.broadcasted_iota(jnp.int32, (size, size), 1)
    eye = row == col
    one = jnp.where(eye, 1.0, 0.0).astype(F32)
    wide = square.astype(F32)
    diagonal = jnp.where(eye, wide, 0.0)
    down = 1.0 / jnp.sum(diagonal, axis=1, keepdims=True)
    across = 1.0 / jnp.sum(diagonal, axis=0, keepdims=True)
    power = jnp.where(eye, 0.0, -wide * down)
    series = one + power
    for _ in range(4):
        low = power.astype(BF16)
        power = dot(low, low)
        series = series + dot(series.astype(BF16), power.astype(BF16))
    guess = series * across
    twice = jnp.concatenate([square, square], axis=1)
    for _ in range(2):
        high, low = split(guess)
        residual = one - dot(twice, jnp.concatenate([high, low], axis=0))
        guess = guess + dot(high, residual.astype(BF16))
    return guess


def kernel(
    sizes,
    counts_ref, slots_ref, walk_hbm, draws_hbm, points_hbm, chol_hbm,
    out_ref, shift_ref,
    walk, draws, pts, back_pts, chol, xsend, stash, selected, xrecv, gbar32, gsend, grecv, gwide,
    gmat, psum32, psend, precv, proj, scaled, term, total, weight,
    load_sem, points_sem, a_send, a_recv, b_send, b_recv, c_send, c_recv, d_send, d_recv,
):
    n, tiles, electrons, orbitals, npts, prow = sizes
    me = lax.axis_index("vec")
    group = lax.axis_index("groups")
    row_tiles = electrons // ROWS
    col_tiles = -(-orbitals // LANES)
    pieces = npts // LANES
    width = tiles * LANES
    chunk = math.gcd(npts, 512)
    chunks = [slice(low, low + chunk) for low in range(0, npts, chunk)]

    load_walk = pltpu.make_async_copy(walk_hbm.at[0], walk, load_sem.at[0])
    load_walk.start()
    load_points = [
        pltpu.make_async_copy(points_hbm.at[:, at], pts.at[:, at], points_sem.at[c])
        for c, at in enumerate(chunks)
    ]
    for load in load_points:
        load.start()
    load_chol = pltpu.make_async_copy(chol_hbm, chol, load_sem.at[1])
    load_chol.start()
    load_draws = pltpu.make_async_copy(draws_hbm, draws, load_sem.at[2])
    load_draws.start()

    barrier = pltpu.get_barrier_semaphore()

    def greet(step, carry):
        pl.semaphore_signal(
            barrier, inc=1, device_id=(group, lax.rem(me + step, n)), device_id_type=MESH
        )
        return carry

    lax.fori_loop(1, n, greet, 0)

    lane = lax.broadcasted_iota(jnp.int32, (ROWS, LANES), 1)
    meta = jnp.where(lane < LANES // 2, counts_ref[0], slots_ref[0]).astype(F32).astype(BF16)
    load_walk.wait()
    for relay in range(n):
        for t in range(tiles):
            tile = relay * tiles + t
            if tile < row_tiles * col_tiles:
                r, c = tile // col_tiles, tile % col_tiles
                low, high = c * LANES, min(orbitals, (c + 1) * LANES)
                block = walk[r * ROWS:(r + 1) * ROWS, low:high]
                if high - low < LANES:
                    block = jnp.concatenate(
                        [block, jnp.zeros((ROWS, LANES - (high - low)), BF16)], axis=1
                    )
                xsend[relay, :, t * LANES:(t + 1) * LANES] = block
            else:
                xsend[relay, :, t * LANES:(t + 1) * LANES] = jnp.zeros((ROWS, LANES), BF16)
        xsend[relay, :, width:] = meta

    inverse = inverse_of(walk[:, :electrons])
    inv_high, inv_low = split(inverse)
    stacked = jnp.concatenate([inv_high, inv_high, inv_low], axis=1)

    def copies(source, target, send_sem, recv_sem):
        def make(step):
            peer = lax.rem(me + step, n)
            return pltpu.make_async_remote_copy(
                src_ref=source(peer), dst_ref=target.at[me],
                send_sem=send_sem.at[step], recv_sem=recv_sem.at[step],
                device_id=(group, peer), device_id_type=MESH,
            )

        return make

    copy_a = copies(lambda peer: xsend.at[peer], stash, a_send, a_recv)
    copy_b = copies(lambda peer: gsend, grecv, b_send, b_recv)
    copy_c = copies(lambda peer: psend.at[peer], precv, c_send, c_recv)
    copy_d = copies(lambda peer: selected.at[peer], xrecv, d_send, d_recv)

    def each(act):
        def body(step, carry):
            act(step)
            return carry

        lax.fori_loop(1, n, body, 0)

    pl.semaphore_wait(barrier, n - 1)
    each(lambda step: copy_a(step).start())
    stash[me] = xsend[me]

    gbar32[...] = jnp.zeros_like(gbar32)
    for c, at in enumerate(chunks):
        load_points[c].wait()
        high, low = split(dot(walk[...], pts[:, at]))
        theta_points = dot(stacked, jnp.concatenate([high, low, high], axis=0))
        density = jnp.sum(
            theta_points * pts[:electrons, at].astype(F32), axis=0, keepdims=True
        )
        for j in range(chunk // LANES):
            k = c * (chunk // LANES) + j
            gbar32[k:k + 1, :] = density[:, j * LANES:(j + 1) * LANES]
    gsend[...] = gbar32[...].astype(BF16)
    each(lambda step: copy_b(step).start())
    grecv[me] = gsend[...]

    each(lambda step: copy_a(step).wait_recv())
    big = n * ROWS
    shift = ROWS.bit_length() - 1
    held = stash[...].reshape(big, width + LANES)
    count_rows = held[:, width:]
    i0 = lax.broadcasted_iota(jnp.int32, (big, big), 0)
    i1 = lax.broadcasted_iota(jnp.int32, (big, big), 1)
    w0, w1 = i0 >> shift, i1 >> shift
    r0, r1 = i0 & (ROWS - 1), i1 & (ROWS - 1)
    before = jnp.where((w1 <= w0) & (r1 == 0), 1.0, 0.0).astype(BF16)
    ends = dot(before, count_rows)[:, :1]
    slot_col = count_rows[:, LANES // 2:LANES // 2 + 1].astype(F32)
    place = w0.astype(F32)

    def source_of(wanted, first, spot):
        copy_row = jnp.sum(
            jnp.where(first & (slot_col == wanted), spot, 0.0), axis=0, keepdims=True
        )
        return jnp.sum(jnp.where(first & (ends <= copy_row), 1.0, 0.0), axis=0, keepdims=True)

    source = source_of(w1.astype(F32), r0 == 0, place)
    pick = jnp.where((place == source) & (r0 == r1), 1.0, 0.0).astype(BF16)
    chosen = dot_tn(pick, held[:, :width]).astype(BF16)
    selected[...] = chosen.reshape(n, ROWS, width)
    each(lambda step: copy_d(step).start())
    xrecv[me] = selected[me]

    k0 = lax.broadcasted_iota(jnp.int32, (big, n), 0)
    k1 = lax.broadcasted_iota(jnp.int32, (big, n), 1)
    thin = source_of(
        k1.astype(F32), (k0 & (ROWS - 1)) == 0, (k0 >> shift).astype(F32)
    )
    walker_row = lax.broadcasted_iota(jnp.int32, (n, n), 0).astype(F32)
    thin_pick = jnp.where(walker_row == thin, 1.0, 0.0).astype(BF16)

    for at in chunks[:3]:
        back_pts[at, :] = pts[:, at].T

    load_chol.wait()
    load_draws.wait()
    each(lambda step: copy_b(step).wait_recv())
    gwide[...] = grecv[...].astype(F32).reshape(n * prow, LANES)
    for j in range(pieces):
        gmat[:, j * LANES:(j + 1) * LANES] = gwide[pl.ds(j, n, stride=prow), :].astype(BF16)
    shifts = jnp.clip(dot_nt(gmat[...], chol[...]), -1.0, 1.0)
    shift_ref[...] = shifts
    fields = (draws[...] - shifts).astype(BF16)
    fields = dot_tn(thin_pick, fields).astype(BF16)
    psum32[...] = jnp.zeros_like(psum32)
    for c, at in enumerate(chunks):
        part = dot(fields, chol[:, at])
        for j in range(chunk // LANES):
            k = c * (chunk // LANES) + j
            psum32[pl.ds(k, n, stride=prow), :] = part[:, j * LANES:(j + 1) * LANES]
    psend[...] = psum32[...].reshape(n, prow, LANES).astype(BF16)
    each(lambda step: copy_c(step).start())
    precv[me] = psend[me]

    each(lambda step: copy_d(step).wait_recv())
    for tile in range(row_tiles * col_tiles):
        relay, t = tile // tiles, tile % tiles
        r, c = tile // col_tiles, tile % col_tiles
        low, high = c * LANES, min(orbitals, (c + 1) * LANES)
        term[r * ROWS:(r + 1) * ROWS, low:high] = (
            xrecv[relay, :, t * LANES:t * LANES + high - low]
        )
    total[...] = term[...].astype(F32)

    def project():
        for at in chunks:
            proj[:, at] = dot(term[...], pts[:, at])

    def scale():
        for j in range(pieces):
            at = slice(j * LANES, (j + 1) * LANES)
            scaled[:, at] = (proj[:, at] * weight[j:j + 1, :]).astype(BF16)

    def back(k):
        for low in range(0, orbitals, 512):
            high = min(orbitals, low + 512)
            value = dot(scaled[...], back_pts[:, low:high]) / k
            total[:, low:high] = total[:, low:high] + value
            term[:, low:high] = value.astype(BF16)

    project()
    for at in chunks[3:]:
        back_pts[at, :] = pts[:, at].T

    each(lambda step: copy_c(step).wait_recv())
    weight[...] = TAU_ROOT * jnp.sum(precv[...].astype(F32), axis=0)

    def taylor(k, carry):
        scale()
        back(k.astype(F32))
        project()
        return carry

    lax.fori_loop(1, ORDER, taylor, 0)
    scale()
    back(float(ORDER))
    out_ref[0] = total[...].astype(BF16)

    for make in (copy_a, copy_b, copy_c, copy_d):
        each(lambda step: make(step).wait_send())


def local(walkers, points, cholesky, field_draws, counts, slot_map):
    n = lax.axis_size("vec")
    walk_rows, electrons, orbitals = walkers.shape
    assert walk_rows == 1 and electrons % ROWS == 0
    npts = points.shape[1]
    tile_count = (electrons // ROWS) * (-(-orbitals // LANES))
    tiles = -(-tile_count // n)
    pieces = npts // LANES
    prow = -(-pieces // ROWS) * ROWS
    sizes = (n, tiles, electrons, orbitals, npts, prow)
    width = tiles * LANES
    vmem = pl.BlockSpec(memory_space=pltpu.VMEM)
    smem = pl.BlockSpec(memory_space=pltpu.SMEM)
    hbm = pl.BlockSpec(memory_space=pl.ANY)
    dma = pltpu.SemaphoreType.DMA
    f32 = lambda *shape: pltpu.VMEM(shape, F32)
    bf16 = lambda *shape: pltpu.VMEM(shape, BF16)
    return pl.pallas_call(
        functools.partial(kernel, sizes),
        out_shape=(
            jax.ShapeDtypeStruct(walkers.shape, BF16),
            jax.ShapeDtypeStruct(field_draws.shape, F32),
        ),
        in_specs=[smem, smem, hbm, hbm, hbm, hbm],
        out_specs=(vmem, vmem),
        scratch_shapes=[
            bf16(electrons, orbitals),
            f32(*field_draws.shape),
            bf16(*points.shape),
            bf16(npts, orbitals),
            bf16(*cholesky.shape),
            bf16(n, ROWS, width + LANES),
            bf16(n, ROWS, width + LANES),
            bf16(n, ROWS, width),
            bf16(n, ROWS, width),
            f32(prow, LANES),
            bf16(prow, LANES),
            bf16(n, prow, LANES),
            f32(n * prow, LANES),
            bf16(n, npts),
            f32(n * prow, LANES),
            bf16(n, prow, LANES),
            bf16(n, prow, LANES),
            f32(electrons, npts),
            bf16(electrons, npts),
            bf16(electrons, orbitals),
            f32(electrons, orbitals),
            f32(prow, LANES),
            dma((3,)),
            dma((npts // math.gcd(npts, 512),)),
        ] + [dma((n,))] * 8,
        compiler_params=pltpu.CompilerParams(
            collective_id=0, has_side_effects=True, vmem_limit_bytes=60 * 1024 * 1024
        ),
        cost_estimate=pl.CostEstimate(
            flops=2 * electrons * orbitals * npts * 9 + 4 * cholesky.size * n,
            bytes_accessed=2 * (points.size + cholesky.size),
            transcendentals=0,
        ),
    )(counts, slot_map, walkers, field_draws, points, cholesky)


def solution(mesh):
    placed = (
        P(("groups", "vec"), None, None),
        P("groups", None),
        P(("groups", "vec"), None),
        P("groups", "vec"),
        P(("groups", "vec")),
        P(("groups", "vec")),
    )
    return jax.shard_map(
        local,
        mesh=mesh,
        in_specs=placed,
        out_specs=(P(("groups", "vec"), None, None), P("groups", "vec")),
        check_vma=False,
    )
```

```python
import functools
import math

import jax
import jax.numpy as jnp
from jax import lax
from jax.experimental import pallas as pl
from jax.experimental.pallas import tpu as pltpu
from jax.sharding import PartitionSpec as P

ORDER = 4
TAU_ROOT = 0.03
LANES = 128
ROWS = 16
F32 = jnp.float32
BF16 = jnp.bfloat16
MESH = pl.DeviceIdType.MESH


def dot(a, b):
    return lax.dot_general(a, b, (((1,), (0,)), ((), ())), preferred_element_type=F32)


def dot_nt(a, b):
    return lax.dot_general(a, b, (((1,), (1,)), ((), ())), preferred_element_type=F32)


def dot_tn(a, b):
    return lax.dot_general(a, b, (((0,), (0,)), ((), ())), preferred_element_type=F32)


def split(value):
    high = value.astype(BF16)
    return high, (value - high.astype(F32)).astype(BF16)


def inverse_of(square):
    size = square.shape[0]
    row = lax.broadcasted_iota(jnp.int32, (size, size), 0)
    col = lax.broadcasted_iota(jnp.int32, (size, size), 1)
    eye = row == col
    one = jnp.where(eye, 1.0, 0.0).astype(F32)
    wide = square.astype(F32)
    diagonal = jnp.where(eye, wide, 0.0)
    down = 1.0 / jnp.sum(diagonal, axis=1, keepdims=True)
    across = 1.0 / jnp.sum(diagonal, axis=0, keepdims=True)
    power = jnp.where(eye, 0.0, -wide * down)
    series = one + power
    for _ in range(4):
        low = power.astype(BF16)
        power = dot(low, low)
        series = series + dot(series.astype(BF16), power.astype(BF16))
    guess = series * across
    twice = jnp.concatenate([square, square], axis=1)
    for _ in range(2):
        high, low = split(guess)
        residual = one - dot(twice, jnp.concatenate([high, low], axis=0))
        guess = guess + dot(high, residual.astype(BF16))
    return guess


def kernel(
    sizes,
    counts_hbm, slots_hbm, walk_hbm, draws_hbm, points_hbm, chol_hbm,
    out_ref, shift_ref,
    walk, draws, pts, back_pts, chol, xsend, stash, selected, xrecv, gbar32, gsend, grecv, gwide,
    gmat, psum32, psend, precv, proj, scaled, term, total, weight,
    counts_ref, slots_ref, load_sem, points_sem, send_sem, recv_sem,
):
    n, tiles, electrons, orbitals, npts, prow = sizes
    me = lax.axis_index("vec")
    group = lax.axis_index("groups")
    row_tiles = electrons // ROWS
    col_tiles = -(-orbitals // LANES)
    pieces = npts // LANES
    width = tiles * LANES
    chunk = math.gcd(npts, 512)
    chunks = [slice(low, low + chunk) for low in range(0, npts, chunk)]

    load_walk = pltpu.make_async_copy(walk_hbm.at[0], walk, load_sem.at[0])
    load_walk.start()
    load_counts = pltpu.make_async_copy(counts_hbm, counts_ref, load_sem.at[3])
    load_counts.start()
    load_slots = pltpu.make_async_copy(slots_hbm, slots_ref, load_sem.at[4])
    load_slots.start()
    load_points = [
        pltpu.make_async_copy(points_hbm.at[:, at], pts.at[:, at], points_sem.at[c])
        for c, at in enumerate(chunks)
    ]
    for load in load_points:
        load.start()
    load_chol = pltpu.make_async_copy(chol_hbm, chol, load_sem.at[1])
    load_chol.start()
    load_draws = pltpu.make_async_copy(draws_hbm, draws, load_sem.at[2])
    load_draws.start()

    barrier = pltpu.get_barrier_semaphore()

    def greet(step, carry):
        pl.semaphore_signal(
            barrier, inc=1, device_id=(group, lax.rem(me + step, n)), device_id_type=MESH
        )
        return carry

    lax.fori_loop(1, n, greet, 0, unroll=n <= 16)

    load_counts.wait()
    load_slots.wait()
    lane = lax.broadcasted_iota(jnp.int32, (ROWS, LANES), 1)
    meta = jnp.where(lane < LANES // 2, counts_ref[0], slots_ref[0]).astype(F32).astype(BF16)
    load_walk.wait()
    for relay in range(n):
        for t in range(tiles):
            tile = relay * tiles + t
            if tile < row_tiles * col_tiles:
                r, c = tile // col_tiles, tile % col_tiles
                low, high = c * LANES, min(orbitals, (c + 1) * LANES)
                block = walk[r * ROWS:(r + 1) * ROWS, low:high]
                if high - low < LANES:
                    block = jnp.concatenate(
                        [block, jnp.zeros((ROWS, LANES - (high - low)), BF16)], axis=1
                    )
                xsend[relay, :, t * LANES:(t + 1) * LANES] = block
            else:
                xsend[relay, :, t * LANES:(t + 1) * LANES] = jnp.zeros((ROWS, LANES), BF16)
        xsend[relay, :, width:] = meta

    class Exchange:
        def __init__(self, source, target, index):
            self.source, self.target = source, target
            self.sems = dict(send_sem=send_sem.at[index], recv_sem=recv_sem.at[index])

        def start(self):
            def body(step, carry):
                peer = lax.rem(me + step, n)
                pltpu.make_async_remote_copy(
                    src_ref=self.source(peer), dst_ref=self.target.at[me],
                    device_id=(group, peer), device_id_type=MESH, **self.sems,
                ).start()
                return carry

            lax.fori_loop(1, n, body, 0, unroll=n <= 16)

        def all_of_them(self):
            return pltpu.make_async_remote_copy(
                src_ref=self.target.at[pl.ds(0, n - 1)], dst_ref=self.target.at[pl.ds(0, n - 1)],
                device_id=(group, lax.rem(me + 1, n)), device_id_type=MESH, **self.sems,
            )

    copy_a = Exchange(lambda peer: xsend.at[peer], stash, 0)
    copy_b = Exchange(lambda peer: gsend, grecv, 1)
    copy_c = Exchange(lambda peer: psend.at[peer], precv, 2)
    copy_d = Exchange(lambda peer: selected.at[peer], xrecv, 3)

    pl.semaphore_wait(barrier, n - 1)
    copy_a.start()
    stash[me] = xsend[me]

    inverse = inverse_of(walk[:, :electrons])
    inv_high, inv_low = split(inverse)
    stacked = jnp.concatenate([inv_high, inv_high, inv_low], axis=1)

    for c, at in enumerate(chunks):
        load_points[c].wait()
        high, low = split(dot(walk[...], pts[:, at]))
        theta_points = dot(stacked, jnp.concatenate([high, low, high], axis=0))
        density = jnp.sum(
            theta_points * pts[:electrons, at].astype(F32), axis=0, keepdims=True
        )
        for j in range(chunk // LANES):
            k = c * (chunk // LANES) + j
            gbar32[k:k + 1, :] = density[:, j * LANES:(j + 1) * LANES]
    gsend[...] = gbar32[...].astype(BF16)
    copy_b.start()
    grecv[me] = gsend[...]

    copy_a.all_of_them().wait_recv()
    big = n * ROWS
    shift = ROWS.bit_length() - 1
    held = stash[...].reshape(big, width + LANES)
    count_rows = held[:, width:]
    i0 = lax.broadcasted_iota(jnp.int32, (big, big), 0)
    i1 = lax.broadcasted_iota(jnp.int32, (big, big), 1)
    w0, w1 = i0 >> shift, i1 >> shift
    r0, r1 = i0 & (ROWS - 1), i1 & (ROWS - 1)
    before = jnp.where((w1 <= w0) & (r1 == 0), 1.0, 0.0).astype(BF16)
    ends = dot(before, count_rows)[:, :1]
    slot_col = count_rows[:, LANES // 2:LANES // 2 + 1].astype(F32)
    place = w0.astype(F32)

    def source_of(wanted, first, spot):
        copy_row = jnp.sum(
            jnp.where(first & (slot_col == wanted), spot, 0.0), axis=0, keepdims=True
        )
        return jnp.sum(jnp.where(first & (ends <= copy_row), 1.0, 0.0), axis=0, keepdims=True)

    source = source_of(w1.astype(F32), r0 == 0, place)
    pick = jnp.where((place == source) & (r0 == r1), 1.0, 0.0).astype(BF16)
    chosen = dot_tn(pick, held[:, :width]).astype(BF16)
    selected[...] = chosen.reshape(n, ROWS, width)

    k0 = lax.broadcasted_iota(jnp.int32, (big, n), 0)
    k1 = lax.broadcasted_iota(jnp.int32, (big, n), 1)
    thin = source_of(
        k1.astype(F32), (k0 & (ROWS - 1)) == 0, (k0 >> shift).astype(F32)
    )
    walker_row = lax.broadcasted_iota(jnp.int32, (n, n), 0).astype(F32)
    thin_pick = jnp.where(walker_row == thin, 1.0, 0.0).astype(BF16)

    for at in chunks[:3]:
        back_pts[at, :] = pts[:, at].T

    load_chol.wait()
    load_draws.wait()
    copy_b.all_of_them().wait_recv()
    copy_d.start()
    xrecv[me] = selected[me]
    for w in range(n):
        gwide[w * prow:w * prow + pieces, :] = grecv[w].astype(F32)
    for j in range(pieces):
        gmat[:, j * LANES:(j + 1) * LANES] = gwide[pl.ds(j, n, stride=prow), :].astype(BF16)
    shifts = jnp.clip(dot_nt(gmat[...], chol[...]), -1.0, 1.0)
    shift_ref[...] = shifts
    fields = (draws[...] - shifts).astype(BF16)
    fields = dot_tn(thin_pick, fields).astype(BF16)
    for c, at in enumerate(chunks):
        part = dot(fields, chol[:, at])
        for j in range(chunk // LANES):
            k = c * (chunk // LANES) + j
            psum32[pl.ds(k, n, stride=prow), :] = part[:, j * LANES:(j + 1) * LANES]
    for w in range(n):
        psend[w] = psum32[w * prow:w * prow + pieces, :].astype(BF16)
    copy_c.start()
    precv[me] = psend[me]

    copy_d.all_of_them().wait_recv()
    for tile in range(row_tiles * col_tiles):
        relay, t = tile // tiles, tile % tiles
        r, c = tile // col_tiles, tile % col_tiles
        low, high = c * LANES, min(orbitals, (c + 1) * LANES)
        term[r * ROWS:(r + 1) * ROWS, low:high] = (
            xrecv[relay, :, t * LANES:t * LANES + high - low]
        )
    total[...] = term[...].astype(F32)

    def project():
        for at in chunks:
            proj[:, at] = dot(term[...], pts[:, at])

    def scale():
        for j in range(pieces):
            at = slice(j * LANES, (j + 1) * LANES)
            scaled[:, at] = (proj[:, at] * weight[j:j + 1, :]).astype(BF16)

    def back(k):
        for low in range(0, orbitals, 512):
            high = min(orbitals, low + 512)
            value = dot(scaled[...], back_pts[:, low:high]) / k
            total[:, low:high] = total[:, low:high] + value
            term[:, low:high] = value.astype(BF16)

    project()
    for at in chunks[3:]:
        back_pts[at, :] = pts[:, at].T

    copy_c.all_of_them().wait_recv()
    weight[...] = TAU_ROOT * jnp.sum(precv[...].astype(F32), axis=0)

    def taylor(k, carry):
        scale()
        back(k.astype(F32))
        project()
        return carry

    lax.fori_loop(1, ORDER, taylor, 0)
    scale()
    back(float(ORDER))
    out_ref[0] = total[...].astype(BF16)

    for copy in (copy_a, copy_b, copy_c, copy_d):
        copy.all_of_them().wait_send()


def local(walkers, points, cholesky, field_draws, counts, slot_map):
    n = lax.axis_size("vec")
    walk_rows, electrons, orbitals = walkers.shape
    assert walk_rows == 1 and electrons % ROWS == 0
    npts = points.shape[1]
    tile_count = (electrons // ROWS) * (-(-orbitals // LANES))
    tiles = -(-tile_count // n)
    pieces = npts // LANES
    prow = -(-pieces // 8) * 8
    sizes = (n, tiles, electrons, orbitals, npts, prow)
    width = tiles * LANES
    vmem = pl.BlockSpec(memory_space=pltpu.VMEM)
    hbm = pl.BlockSpec(memory_space=pltpu.HBM)
    dma = pltpu.SemaphoreType.DMA
    f32 = lambda *shape: pltpu.VMEM(shape, F32)
    bf16 = lambda *shape: pltpu.VMEM(shape, BF16)
    return pl.pallas_call(
        functools.partial(kernel, sizes),
        out_shape=(
            pltpu.VMEM(walkers.shape, BF16),
            pltpu.VMEM(field_draws.shape, F32),
        ),
        in_specs=[hbm, hbm, hbm, hbm, hbm, hbm],
        out_specs=(vmem, vmem),
        scratch_shapes=[
            bf16(electrons, orbitals),
            f32(*field_draws.shape),
            bf16(*points.shape),
            bf16(npts, orbitals),
            bf16(*cholesky.shape),
            bf16(n, ROWS, width + LANES),
            bf16(n, ROWS, width + LANES),
            bf16(n, ROWS, width),
            bf16(n, ROWS, width),
            f32(pieces, LANES),
            bf16(pieces, LANES),
            bf16(n, pieces, LANES),
            f32(n * prow, LANES),
            bf16(n, npts),
            f32(n * prow, LANES),
            bf16(n, pieces, LANES),
            bf16(n, pieces, LANES),
            f32(electrons, npts),
            bf16(electrons, npts),
            bf16(electrons, orbitals),
            f32(electrons, orbitals),
            f32(pieces, LANES),
            pltpu.SMEM((1,), jnp.int32),
            pltpu.SMEM((1,), jnp.int32),
            dma((5,)),
            dma((npts // math.gcd(npts, 512),)),
            dma((4,)),
            dma((4,)),
        ],
        compiler_params=pltpu.CompilerParams(
            collective_id=0, has_side_effects=True, vmem_limit_bytes=60 * 1024 * 1024
        ),
        cost_estimate=pl.CostEstimate(
            flops=2 * electrons * orbitals * npts * 9 + 4 * cholesky.size * n,
            bytes_accessed=2 * (points.size + cholesky.size),
            transcendentals=0,
        ),
    )(counts, slot_map, walkers, field_draws, points, cholesky)


def solution(mesh):
    placed = (
        P(("groups", "vec"), None, None),
        P("groups", None),
        P(("groups", "vec"), None),
        P("groups", "vec"),
        P(("groups", "vec")),
        P(("groups", "vec")),
    )
    return jax.shard_map(
        local,
        mesh=mesh,
        in_specs=placed,
        out_specs=(P(("groups", "vec"), None, None), P("groups", "vec")),
        check_vma=False,
    )
```

```python
import functools
import math

import jax
import jax.numpy as jnp
from jax import lax
from jax.experimental import pallas as pl
from jax.experimental.pallas import tpu as pltpu
from jax.sharding import PartitionSpec as P

ORDER = 4
TAU_ROOT = 0.03
LANES = 128
ROWS = 16
F32 = jnp.float32
BF16 = jnp.bfloat16
MESH = pl.DeviceIdType.MESH


def dot(a, b):
    return lax.dot_general(a, b, (((1,), (0,)), ((), ())), preferred_element_type=F32)


def dot_nt(a, b):
    return lax.dot_general(a, b, (((1,), (1,)), ((), ())), preferred_element_type=F32)


def dot_tn(a, b):
    return lax.dot_general(a, b, (((0,), (0,)), ((), ())), preferred_element_type=F32)


def split(value):
    high = value.astype(BF16)
    return high, (value - high.astype(F32)).astype(BF16)


def inverse_of(square):
    size = square.shape[0]
    row = lax.broadcasted_iota(jnp.int32, (size, size), 0)
    col = lax.broadcasted_iota(jnp.int32, (size, size), 1)
    eye = row == col
    one = jnp.where(eye, 1.0, 0.0).astype(F32)
    wide = square.astype(F32)
    diagonal = jnp.where(eye, wide, 0.0)
    down = 1.0 / jnp.sum(diagonal, axis=1, keepdims=True)
    across = 1.0 / jnp.sum(diagonal, axis=0, keepdims=True)
    power = jnp.where(eye, 0.0, -wide * down)
    series = one + power
    for _ in range(4):
        low = power.astype(BF16)
        power = dot(low, low)
        series = series + dot(series.astype(BF16), power.astype(BF16))
    guess = series * across
    twice = jnp.concatenate([square, square], axis=1)
    for _ in range(2):
        high, low = split(guess)
        residual = one - dot(twice, jnp.concatenate([high, low], axis=0))
        guess = guess + dot(high, residual.astype(BF16))
    return guess


def kernel(
    sizes,
    counts_hbm, slots_hbm, walk_hbm, draws_hbm, points_hbm, chol_hbm,
    out_ref, shift_ref,
    walk, draws, pts, back_pts, chol, xsend, stash, selected, xrecv, gbar32, gsend, grecv, gwide,
    gmat, psum32, psend, precv, proj, scaled, term, total, weight,
    counts_ref, slots_ref, load_sem, points_sem, send_sem, recv_sem,
):
    n, tiles, electrons, orbitals, npts, prow = sizes
    me = lax.axis_index("vec")
    group = lax.axis_index("groups")
    row_tiles = electrons // ROWS
    col_tiles = -(-orbitals // LANES)
    pieces = npts // LANES
    width = tiles * LANES
    chunk = math.gcd(npts, 512)
    chunks = [slice(low, low + chunk) for low in range(0, npts, chunk)]

    load_walk = pltpu.make_async_copy(walk_hbm.at[0], walk, load_sem.at[0])
    load_walk.start()
    load_counts = pltpu.make_async_copy(counts_hbm, counts_ref, load_sem.at[3])
    load_counts.start()
    load_slots = pltpu.make_async_copy(slots_hbm, slots_ref, load_sem.at[4])
    load_slots.start()
    load_points = [
        pltpu.make_async_copy(points_hbm.at[:, at], pts.at[:, at], points_sem.at[c])
        for c, at in enumerate(chunks)
    ]
    for load in load_points:
        load.start()
    load_chol = pltpu.make_async_copy(chol_hbm, chol, load_sem.at[1])
    load_chol.start()
    load_draws = pltpu.make_async_copy(draws_hbm, draws, load_sem.at[2])
    load_draws.start()

    barrier = pltpu.get_barrier_semaphore()

    def greet(step, carry):
        pl.semaphore_signal(
            barrier, inc=1, device_id=(group, lax.rem(me + step, n)), device_id_type=MESH
        )
        return carry

    lax.fori_loop(1, n, greet, 0, unroll=n <= 16)

    load_counts.wait()
    load_slots.wait()
    lane = lax.broadcasted_iota(jnp.int32, (ROWS, LANES), 1)
    meta = jnp.where(lane < LANES // 2, counts_ref[0], slots_ref[0]).astype(F32).astype(BF16)
    load_walk.wait()
    for relay in range(n):
        for t in range(tiles):
            tile = relay * tiles + t
            if tile < row_tiles * col_tiles:
                r, c = tile // col_tiles, tile % col_tiles
                low, high = c * LANES, min(orbitals, (c + 1) * LANES)
                block = walk[r * ROWS:(r + 1) * ROWS, low:high]
                if high - low < LANES:
                    block = jnp.concatenate(
                        [block, jnp.zeros((ROWS, LANES - (high - low)), BF16)], axis=1
                    )
                xsend[relay, :, t * LANES:(t + 1) * LANES] = block
            else:
                xsend[relay, :, t * LANES:(t + 1) * LANES] = jnp.zeros((ROWS, LANES), BF16)
        xsend[relay, :, width:] = meta

    class Exchange:
        def __init__(self, source, target, index):
            self.source, self.target = source, target
            self.sems = dict(send_sem=send_sem.at[index], recv_sem=recv_sem.at[index])

        def start(self):
            def body(step, carry):
                far_first = lax.rem(step + n // 2 - 2, n - 1) + 1
                peer = lax.rem(me + far_first, n)
                pltpu.make_async_remote_copy(
                    src_ref=self.source(peer), dst_ref=self.target.at[me],
                    device_id=(group, peer), device_id_type=MESH, **self.sems,
                ).start()
                return carry

            lax.fori_loop(1, n, body, 0, unroll=n <= 16)

        def all_of_them(self):
            return pltpu.make_async_remote_copy(
                src_ref=self.target.at[pl.ds(0, n - 1)], dst_ref=self.target.at[pl.ds(0, n - 1)],
                device_id=(group, lax.rem(me + 1, n)), device_id_type=MESH, **self.sems,
            )

    copy_a = Exchange(lambda peer: xsend.at[peer], stash, 0)
    copy_b = Exchange(lambda peer: gsend, grecv, 1)
    copy_c = Exchange(lambda peer: psend.at[peer], precv, 2)
    copy_d = Exchange(lambda peer: selected.at[peer], xrecv, 3)

    pl.semaphore_wait(barrier, n - 1)
    copy_a.start()
    stash[me] = xsend[me]

    inverse = inverse_of(walk[:, :electrons])
    inv_high, inv_low = split(inverse)
    stacked = jnp.concatenate([inv_high, inv_high, inv_low], axis=1)

    for c, at in enumerate(chunks):
        load_points[c].wait()
        high, low = split(dot(walk[...], pts[:, at]))
        theta_points = dot(stacked, jnp.concatenate([high, low, high], axis=0))
        density = jnp.sum(
            theta_points * pts[:electrons, at].astype(F32), axis=0, keepdims=True
        )
        for j in range(chunk // LANES):
            k = c * (chunk // LANES) + j
            gbar32[k:k + 1, :] = density[:, j * LANES:(j + 1) * LANES]
    gsend[...] = gbar32[...].astype(BF16)
    copy_b.start()
    grecv[me] = gsend[...]

    copy_a.all_of_them().wait_recv()
    big = n * ROWS
    shift = ROWS.bit_length() - 1
    held = stash[...].reshape(big, width + LANES)
    count_rows = held[:, width:]
    i0 = lax.broadcasted_iota(jnp.int32, (big, big), 0)
    i1 = lax.broadcasted_iota(jnp.int32, (big, big), 1)
    w0, w1 = i0 >> shift, i1 >> shift
    r0, r1 = i0 & (ROWS - 1), i1 & (ROWS - 1)
    before = jnp.where((w1 <= w0) & (r1 == 0), 1.0, 0.0).astype(BF16)
    ends = dot(before, count_rows)[:, :1]
    slot_col = count_rows[:, LANES // 2:LANES // 2 + 1].astype(F32)
    place = w0.astype(F32)

    def source_of(wanted, first, spot):
        copy_row = jnp.sum(
            jnp.where(first & (slot_col == wanted), spot, 0.0), axis=0, keepdims=True
        )
        return jnp.sum(jnp.where(first & (ends <= copy_row), 1.0, 0.0), axis=0, keepdims=True)

    source = source_of(w1.astype(F32), r0 == 0, place)
    pick = jnp.where((place == source) & (r0 == r1), 1.0, 0.0).astype(BF16)
    chosen = dot_tn(pick, held[:, :width]).astype(BF16)
    selected[...] = chosen.reshape(n, ROWS, width)

    k0 = lax.broadcasted_iota(jnp.int32, (big, n), 0)
    k1 = lax.broadcasted_iota(jnp.int32, (big, n), 1)
    thin = source_of(
        k1.astype(F32), (k0 & (ROWS - 1)) == 0, (k0 >> shift).astype(F32)
    )
    walker_row = lax.broadcasted_iota(jnp.int32, (n, n), 0).astype(F32)
    thin_pick = jnp.where(walker_row == thin, 1.0, 0.0).astype(BF16)

    for at in chunks[:3]:
        back_pts[at, :] = pts[:, at].T

    load_chol.wait()
    load_draws.wait()
    copy_b.all_of_them().wait_recv()
    copy_d.start()
    xrecv[me] = selected[me]
    for w in range(n):
        gwide[w * prow:w * prow + pieces, :] = grecv[w].astype(F32)
    for j in range(pieces):
        gmat[:, j * LANES:(j + 1) * LANES] = gwide[pl.ds(j, n, stride=prow), :].astype(BF16)
    shifts = jnp.clip(dot_nt(gmat[...], chol[...]), -1.0, 1.0)
    shift_ref[...] = shifts
    fields = (draws[...] - shifts).astype(BF16)
    fields = dot_tn(thin_pick, fields).astype(BF16)
    for c, at in enumerate(chunks):
        part = dot(fields, chol[:, at])
        for j in range(chunk // LANES):
            k = c * (chunk // LANES) + j
            psum32[pl.ds(k, n, stride=prow), :] = part[:, j * LANES:(j + 1) * LANES]
    for w in range(n):
        psend[w] = psum32[w * prow:w * prow + pieces, :].astype(BF16)
    copy_c.start()
    precv[me] = psend[me]

    copy_d.all_of_them().wait_recv()
    for tile in range(row_tiles * col_tiles):
        relay, t = tile // tiles, tile % tiles
        r, c = tile // col_tiles, tile % col_tiles
        low, high = c * LANES, min(orbitals, (c + 1) * LANES)
        term[r * ROWS:(r + 1) * ROWS, low:high] = (
            xrecv[relay, :, t * LANES:t * LANES + high - low]
        )
    total[...] = term[...].astype(F32)

    def project():
        for at in chunks:
            proj[:, at] = dot(term[...], pts[:, at])

    def scale():
        for j in range(pieces):
            at = slice(j * LANES, (j + 1) * LANES)
            scaled[:, at] = (proj[:, at] * weight[j:j + 1, :]).astype(BF16)

    def back(k):
        for low in range(0, orbitals, 512):
            high = min(orbitals, low + 512)
            value = dot(scaled[...], back_pts[:, low:high]) / k
            total[:, low:high] = total[:, low:high] + value
            term[:, low:high] = value.astype(BF16)

    project()
    for at in chunks[3:]:
        back_pts[at, :] = pts[:, at].T

    copy_c.all_of_them().wait_recv()
    weight[...] = TAU_ROOT * jnp.sum(precv[...].astype(F32), axis=0)

    def taylor(k, carry):
        scale()
        back(k.astype(F32))
        project()
        return carry

    lax.fori_loop(1, ORDER, taylor, 0)
    scale()
    back(float(ORDER))
    out_ref[0] = total[...].astype(BF16)

    for copy in (copy_a, copy_b, copy_c, copy_d):
        copy.all_of_them().wait_send()


def local(walkers, points, cholesky, field_draws, counts, slot_map):
    n = lax.axis_size("vec")
    walk_rows, electrons, orbitals = walkers.shape
    assert walk_rows == 1 and electrons % ROWS == 0
    npts = points.shape[1]
    tile_count = (electrons // ROWS) * (-(-orbitals // LANES))
    tiles = -(-tile_count // n)
    pieces = npts // LANES
    prow = -(-pieces // 8) * 8
    sizes = (n, tiles, electrons, orbitals, npts, prow)
    width = tiles * LANES
    vmem = pl.BlockSpec(memory_space=pltpu.VMEM)
    hbm = pl.BlockSpec(memory_space=pltpu.HBM)
    dma = pltpu.SemaphoreType.DMA
    f32 = lambda *shape: pltpu.VMEM(shape, F32)
    bf16 = lambda *shape: pltpu.VMEM(shape, BF16)
    return pl.pallas_call(
        functools.partial(kernel, sizes),
        out_shape=(
            pltpu.VMEM(walkers.shape, BF16),
            pltpu.VMEM(field_draws.shape, F32),
        ),
        in_specs=[hbm, hbm, hbm, hbm, hbm, hbm],
        out_specs=(vmem, vmem),
        scratch_shapes=[
            bf16(electrons, orbitals),
            f32(*field_draws.shape),
            bf16(*points.shape),
            bf16(npts, orbitals),
            bf16(*cholesky.shape),
            bf16(n, ROWS, width + LANES),
            bf16(n, ROWS, width + LANES),
            bf16(n, ROWS, width),
            bf16(n, ROWS, width),
            f32(pieces, LANES),
            bf16(pieces, LANES),
            bf16(n, pieces, LANES),
            f32(n * prow, LANES),
            bf16(n, npts),
            f32(n * prow, LANES),
            bf16(n, pieces, LANES),
            bf16(n, pieces, LANES),
            f32(electrons, npts),
            bf16(electrons, npts),
            bf16(electrons, orbitals),
            f32(electrons, orbitals),
            f32(pieces, LANES),
            pltpu.SMEM((1,), jnp.int32),
            pltpu.SMEM((1,), jnp.int32),
            dma((5,)),
            dma((npts // math.gcd(npts, 512),)),
            dma((4,)),
            dma((4,)),
        ],
        compiler_params=pltpu.CompilerParams(
            collective_id=0, has_side_effects=True, vmem_limit_bytes=60 * 1024 * 1024
        ),
        cost_estimate=pl.CostEstimate(
            flops=2 * electrons * orbitals * npts * 9 + 4 * cholesky.size * n,
            bytes_accessed=2 * (points.size + cholesky.size),
            transcendentals=0,
        ),
    )(counts, slot_map, walkers, field_draws, points, cholesky)


def solution(mesh):
    placed = (
        P(("groups", "vec"), None, None),
        P("groups", None),
        P(("groups", "vec"), None),
        P("groups", "vec"),
        P(("groups", "vec")),
        P(("groups", "vec")),
    )
    return jax.shard_map(
        local,
        mesh=mesh,
        in_specs=placed,
        out_specs=(P(("groups", "vec"), None, None), P("groups", "vec")),
        check_vma=False,
    )
```
